32 devices in a mesh: groups: 2 (over x), seq: 16 (over z, y, core).
Axes of the slice: x: 2, y: 2, z: 4, core: 2. Of those that a mesh axis runs over, the one named last changes fastest.
Arguments:
- prompt_kv: bfloat16 [8192, 1024], P(('groups', 'seq')), parts along dimension 0, may hold values from -6 to 6
- prompt_pages: int32 [16], P('groups'), parts along dimension 0, may hold values from 1 to 16, 32 in all
- prompt_slot: int32 [16], P('groups'), parts along dimension 0, may hold values from 0 to 31, as said below
- cache_kv: bfloat16 [256, 2048, 256], P(('groups', 'seq')), parts along dimension 0, may hold values from -6 to 6
- cache_len: int32 [64], P('groups'), parts along dimension 0, may hold values from 1 to 2048
- queries: bfloat16 [64, 4, 8192], P(('groups', 'seq')), parts along dimension 0, may hold values from -72 to 72
- new_kv: bfloat16 [64, 4, 1024], P(('groups', 'seq')), parts along dimension 0, may hold values from -6 to 6
Outputs:
- attended: bfloat16 [64, 4, 8192], P(('groups', 'seq')), parts along dimension 0
The draws below stay inside these ranges and needn't reach their ends.
There are 2 independent parts, one for each index of `groups`. The reference program is written for one: setup_inputs(seed, part) draws one part's arguments, and reference() takes and returns one part's arrays. A program takes and returns all parts, laid end to end along the dimension named above; each array names one. Nothing has to cross between parts.
Inputs may be any that keep to these rules, and one draw needn't show every extreme that they name: `prompt_slot`: distinct decode rows.
All inputs are finite; a program needn't handle non-finite values.
Results may differ from the reference program's by a relative error of at most 0.0061.
Values may be sent and summed in bfloat16 or wider, within the bound.
A program may use at most 128 MiB of HBM per device.

```python
import math
import jax
import jax.numpy as jnp
import numpy as np
from jax import lax

HD = 128
KVH = 4
QPK = 16
PAGE = 128
CTX = 2048
STEPS = 4
ROWS_DEV = 8
NPAGE = 32
PTOK = 4096
NP = 8
MOSTP = 16
B = 32


def draw_prompt_slot(key, part):
    key = jax.random.fold_in(key, 11)
    return jax.random.permutation(key, B)[:NP].astype(jnp.int32)


def draw_queries(key, part):
    key = jax.random.fold_in(key, 5)
    first = jax.random.fold_in(key, 0)
    base = jax.random.truncated_normal(first, -6.0, 6.0, (B, STEPS, KVH * QPK, HD), jnp.float32)
    return base.reshape(B, STEPS, KVH * QPK * HD).astype(jnp.bfloat16)


def set_ends(values, rng, low, largest):
    index_at = [jax.random.randint(jax.random.fold_in(rng, axis), (), 0, length) for axis, length in enumerate(values.shape)]
    widest = values.shape.index(max(values.shape))
    next_to = index_at[:widest] + [(index_at[widest] + 1) % values.shape[widest]] + index_at[widest + 1:]
    return values.at[tuple(index_at)].set(low).at[tuple(next_to)].set(largest)


def shard_levels(rng, dims, shards, least, largest):
    level, own = 1.0, jax.random.fold_in(rng, 6)
    for axis_at, shards_of in shards:
        heights = jnp.exp(jax.random.uniform(jax.random.fold_in(own, axis_at), (shards_of,), jnp.float32, least / len(shards), largest / len(shards)))
        level = level * jnp.repeat(heights, dims[axis_at] // shards_of).reshape([-1 if axis == axis_at else 1 for axis in range(len(dims))])
    return level


def profile(amount, total, most, lean):
    loads = [(1 << 20) // math.isqrt(standing ** lean) + 1 for standing in range(2, amount + 1)]
    spare, holding = total - most - (amount - 1), [1] * (amount - 1)
    while spare > 0:
        candidates = [i for i in range(amount - 1) if holding[i] < most]
        mass, budget = sum([loads[i] for i in candidates]), spare
        for i in candidates:
            addition = min(most - holding[i], max(1, budget * loads[i] // mass), spare)
            holding[i] = holding[i] + addition
            spare = spare - addition
    return np.array([most] + holding)


def uneven_parts(stream_key, number_of, total, most, lean):
    if number_of == 2:
        one = jax.random.randint(stream_key, (), max(1, total - most), min(most, total - 1) + 1)
        return jnp.stack([one, total - one])
    tallies = jnp.asarray(profile(number_of, total, most, lean), jnp.int32)
    pairs = (number_of - 1) // 2
    source_of, taker = tallies[1:1 + 2 * pairs:2], tallies[2:2 + 2 * pairs:2]
    slack = jnp.minimum(source_of - 1, most - taker)
    passed = jax.random.randint(jax.random.fold_in(stream_key, 1), (pairs,), 0, 1 << 20) % (slack + 1)
    tallies = tallies.at[1:1 + 2 * pairs:2].set(source_of - passed).at[2:2 + 2 * pairs:2].set(taker + passed)
    return tallies[jax.random.permutation(jax.random.fold_in(stream_key, 2), number_of)]


def normal_values(key, dims, spread, reach, cuts=(), kind=jnp.bfloat16):
    factor_of = shard_levels(key, dims, cuts, -0.22, 0.18) if cuts else 1.0
    drawn = jax.random.normal(key, dims, jnp.float32) * spread * factor_of
    return jnp.minimum(jnp.maximum(drawn, -reach), reach).astype(kind)


def setup_inputs(seed: int = 0, part: int = 0) -> dict:
    splits = jax.random.split(jax.random.key(seed), 8)
    own_keys = jax.random.split(jax.random.fold_in(splits[7], part), 8)
    prompt_kv = normal_values(own_keys[0], (PTOK, KVH * 2 * HD), 1.0, 6.0, ((0, 16),))
    prompt_pages = uneven_parts(own_keys[1], NP, NPAGE, MOSTP, 2).astype(jnp.int32)
    prompt_slot = draw_prompt_slot(jax.random.fold_in(jax.random.fold_in(splits[7], part), 71), part)
    cache_kv = normal_values(own_keys[3], (KVH * B, CTX, 2 * HD), 1.0, 6.0, ((0, 16),))
    cache_len = set_ends(jax.random.randint(own_keys[4], (B,), 1, CTX + 1), jax.random.fold_in(own_keys[4], 1), 1, CTX).astype(jnp.int32)
    queries = draw_queries(jax.random.fold_in(jax.random.fold_in(splits[7], part), 71), part)
    new_kv = normal_values(own_keys[6], (B, STEPS, KVH * 2 * HD), 1.0, 6.0, ((0, 16),))
    return dict(prompt_kv=prompt_kv, prompt_pages=prompt_pages, prompt_slot=prompt_slot, cache_kv=cache_kv, cache_len=cache_len, queries=queries, new_kv=new_kv)


THETA = 500000.0


def rotate(keys, positions):
    half = keys.shape[-1] // 2
    freq = THETA ** (-(2.0 * jnp.arange(half, dtype=jnp.float32)) / keys.shape[-1])
    angle = positions.astype(jnp.float32)[:, None] * freq[None, :]
    cosine = jnp.cos(angle)[:, None, :]
    sine = jnp.sin(angle)[:, None, :]
    first = keys[..., :half]
    second = keys[..., half:]
    return jnp.concatenate([first * cosine - second * sine, second * cosine + first * sine], axis=-1)


def attend_row(query, context, fresh_kv, length):
    heads = query.reshape(STEPS, QPK, HD).astype(jnp.float32)
    keys = jnp.concatenate([context[:, :HD], fresh_kv[:, :HD]], axis=0).astype(jnp.float32)
    values = jnp.concatenate([context[:, HD:], fresh_kv[:, HD:]], axis=0).astype(jnp.float32)
    scores = jnp.einsum("sjd,cd->sjc", heads, keys) * (HD ** -0.5)
    column = jnp.arange(CTX + STEPS, dtype=jnp.int32)
    step_ids = jnp.arange(STEPS, dtype=jnp.int32)
    valid = jnp.where(column[None, :] < CTX, column[None, :] < length, (column[None, :] - CTX) <= step_ids[:, None])
    scores = jnp.where(valid[:, None, :], scores, -jnp.inf)
    top = jnp.max(scores, axis=-1, keepdims=True)
    expo = jnp.exp(scores - top)
    total = jnp.sum(expo, axis=-1, keepdims=True)
    weights = expo.astype(jnp.bfloat16).astype(jnp.float32)
    out = jnp.einsum("sjc,cd->sjd", weights, values) / total
    return out.reshape(STEPS, QPK * HD).astype(jnp.bfloat16)


def reference(prompt_kv, prompt_pages, prompt_slot, cache_kv, cache_len, queries, new_kv):
    ends = jnp.cumsum(prompt_pages)
    starts = ends - prompt_pages
    page_ids = jnp.arange(NPAGE, dtype=jnp.int32)
    owner = jnp.sum((page_ids[:, None] >= ends[None, :]).astype(jnp.int32), axis=1)
    onehot = (owner[:, None] == jnp.arange(NP, dtype=jnp.int32)[None, :]).astype(jnp.int32)
    page_start = jnp.sum(onehot * starts[None, :], axis=1)
    tokens = jnp.arange(PTOK, dtype=jnp.int32)
    positions = tokens - page_start[tokens // PAGE] * PAGE
    packed = prompt_kv.reshape(PTOK, KVH, 2 * HD)
    rotated = rotate(packed[:, :, :HD].astype(jnp.float32), positions).astype(jnp.bfloat16)
    handed = jnp.concatenate([rotated, packed[:, :, HD:]], axis=-1)
    match = prompt_slot[None, :] == jnp.arange(B, dtype=jnp.int32)[:, None]
    has = jnp.any(match, axis=1)
    slot_start = jnp.sum(match.astype(jnp.int32) * starts[None, :], axis=1)
    slot_len = jnp.sum(match.astype(jnp.int32) * prompt_pages[None, :], axis=1) * PAGE

    def one_row(index):
        head = (index // ROWS_DEV) % KVH
        row = (index // (KVH * ROWS_DEV)) * ROWS_DEV + index % ROWS_DEV
        spots = jnp.clip(slot_start[row] * PAGE + jnp.arange(CTX, dtype=jnp.int32), 0, PTOK - 1)
        fresh = handed[spots, head, :]
        context = jnp.where(has[row], fresh, cache_kv[index])
        length = jnp.where(has[row], slot_len[row], cache_len[row])
        query = lax.dynamic_slice_in_dim(queries[row], head * QPK * HD, QPK * HD, 1)
        fresh_kv = lax.dynamic_slice_in_dim(new_kv[row], head * 2 * HD, 2 * HD, 1)
        return attend_row(query, context, fresh_kv, length)

    outs = lax.map(one_row, jnp.arange(KVH * B, dtype=jnp.int32))
    outs = outs.reshape(B // ROWS_DEV, KVH, ROWS_DEV, STEPS, QPK * HD).transpose(0, 2, 3, 1, 4)
    return outs.reshape(B, STEPS, KVH * QPK * HD)
```

```python
import functools

import jax
import jax.numpy as jnp
from jax import lax
from jax.experimental import pallas as pl
from jax.experimental.pallas import tpu as pltpu
from jax.sharding import PartitionSpec as P

HD = 128
KVH = 4
QPK = 16
PAGE = 128
THETA = 500000.0
LOW = -1e30
MESH = pl.DeviceIdType.MESH
BF = jnp.bfloat16
F32 = jnp.float32


def dot_t(a, b):
    return lax.dot_general(a, b, (((1,), (1,)), ((), ())), preferred_element_type=F32)


def dot(a, b):
    return jnp.dot(a, b, preferred_element_type=F32)


def kernel(
    nseq, steps, per_src, ppd, nprompt, ctx,
    pages_ref, slot_ref, clen_ref, freq_ref, joined_ref, pkv_hbm, cache_hbm,
    out_ref,
    prow, pfirst, plast, rowp,
    pkv, cache, keys, stage1, qall, gq, stage2, q2, stage3, r3, lse, fmax, fsum, facc,
    nmax, nsum, nacc, fin, stage4, r4, res6, r6,
    csem, psem, s1, t1, s2, t2, s3, t3, s4, t4, s5, t5, s6, t6,
):
    nslice = KVH * steps
    npage = ppd * nseq
    rows = KVH * per_src
    qrows = nslice * per_src
    qn = steps * QPK
    scale = HD ** -0.5
    me = lax.axis_index("seq")
    grp = me // KVH
    head = me % KVH
    quad = me // nslice
    mine = me % nslice
    step = mine % steps
    qbase = quad * nslice

    barrier = pltpu.get_barrier_semaphore()

    def greet(k, c):
        pl.semaphore_signal(barrier, inc=1, device_id={"seq": (me + k) % nseq}, device_id_type=MESH)
        return c

    lax.fori_loop(1, nseq, greet, 0)

    load_p = pltpu.make_async_copy(pkv_hbm, pkv, psem)
    load_p.start()

    def load_c(r):
        return pltpu.make_async_copy(cache_hbm.at[r], cache.at[r], csem.at[r])

    for r in range(rows):
        load_c(r).start()

    for h in range(KVH):
        for s in range(steps):
            for r in range(per_src):
                stage1[h * steps + s, r, :QPK] = joined_ref[h, r, s * QPK : (s + 1) * QPK]
                stage1[h * steps + s, r, QPK:] = joined_ref[h, r, qn : qn + 16]

    def page_row(g, c):
        p, start, end = c
        new = g >= end
        p = jnp.minimum(jnp.where(new, p + 1, p), nprompt - 1)
        start = jnp.where(new, end, start)
        end = jnp.where(new, end + pages_ref[p], end)
        prow[g] = slot_ref[p]
        pfirst[g] = start
        return p, start, end

    lax.fori_loop(0, npage, page_row, (jnp.int32(0), jnp.int32(0), pages_ref[0]))

    last = jnp.int32(-1)
    for p in range(nprompt):
        last = last + pages_ref[p]
        plast[p] = jnp.clip(last, 0, npage - 1)

    pl.semaphore_wait(barrier, nseq - 1)

    def c1(t, src):
        return pltpu.make_async_remote_copy(
            src_ref=stage1.at[t % nslice], dst_ref=qall.at[pl.ds(src * per_src, per_src)],
            send_sem=s1.at[t], recv_sem=t1.at[src], device_id={"seq": t}, device_id_type=MESH)

    def c2(t, src):
        return pltpu.make_async_remote_copy(
            src_ref=stage2.at[t], dst_ref=q2.at[src],
            send_sem=s2.at[t], recv_sem=t2.at[src], device_id={"seq": qbase + t}, device_id_type=MESH)

    def c3(t, src):
        return pltpu.make_async_remote_copy(
            src_ref=stage3.at[t % nslice], dst_ref=r3.at[src],
            send_sem=s3.at[t], recv_sem=t3.at[src], device_id={"seq": t}, device_id_type=MESH)

    def c4(t, src):
        return pltpu.make_async_remote_copy(
            src_ref=stage4.at[t], dst_ref=r4.at[src],
            send_sem=s4.at[t], recv_sem=t4.at[src], device_id={"seq": qbase + t}, device_id_type=MESH)

    def c5(t, src):
        return pltpu.make_async_remote_copy(
            src_ref=joined_ref.at[t], dst_ref=gq.at[pl.ds(src * per_src, per_src)],
            send_sem=s5.at[t], recv_sem=t5.at[src], device_id={"seq": grp * KVH + t}, device_id_type=MESH)

    def c6(t, src):
        return pltpu.make_async_remote_copy(
            src_ref=res6.at[pl.ds(t * per_src, per_src)], dst_ref=r6.at[src],
            send_sem=s6.at[t], recv_sem=t6.at[src], device_id={"seq": grp * KVH + t}, device_id_type=MESH)

    def send(copy, n, at):
        def go(k, c):
            copy((at + k) % n, at).start()
            return c
        lax.fori_loop(1, n, go, 0)

    def arrive(copy, n, at):
        def go(k, c):
            copy((at + k) % n, (at + n - k) % n).wait_recv()
            return c
        lax.fori_loop(1, n, go, 0)

    def left(copy, n, at):
        def go(k, c):
            copy((at + k) % n, at).wait_send()
            return c
        lax.fori_loop(1, n, go, 0)

    send(c1, nseq, me)
    send(c5, KVH, head)
    qall[pl.ds(me * per_src, per_src)] = stage1[mine]
    gq[pl.ds(head * per_src, per_src)] = joined_ref[head]

    def row_prompt(r, c):
        found = jnp.int32(-1)
        for p in range(nprompt):
            found = jnp.where(slot_ref[p] == r + quad * qrows, p, found)
        rowp[r] = found
        return c

    lax.fori_loop(0, qrows, row_prompt, 0)

    load_p.wait()
    lane = lax.broadcasted_iota(jnp.int32, (PAGE, HD), 1)
    token = lax.broadcasted_iota(jnp.int32, (PAGE, HD), 0)
    for i in range(ppd):
        page = me * ppd + i
        position = (token + (page - pfirst[page]) * PAGE).astype(F32)
        angle = position * freq_ref[0:1, :]
        cosine = jnp.cos(angle)
        sine = jnp.sin(angle)
        sine = jnp.where(lane < HD // 2, -sine, sine)
        for h in range(KVH):
            key = pkv[i * PAGE : (i + 1) * PAGE, h * 2 * HD : h * 2 * HD + HD].astype(F32)
            keys[i, h] = (key * cosine + pltpu.roll(key, HD // 2, 1) * sine).astype(BF)

    arrive(c1, nseq, me)
    for t in range(nslice):
        for i in range(ppd):
            row = prow[(qbase + t) * ppd + i]
            stage2[t, i] = qall[row, :QPK]
    send(c2, nslice, mine)
    q2[mine] = stage2[mine]

    def fresh(tile, valid, q):
        sc = dot_t(q, tile) * scale
        sc = jnp.where(valid, sc, LOW)
        v = pltpu.roll(tile.astype(F32), 16 - steps, 0).astype(BF)
        return sc, v

    col_n = lax.broadcasted_iota(jnp.int32, (QPK, 16), 1)
    for p in range(nprompt):
        row = slot_ref[p]
        tile = qall[row]
        sc, v = fresh(tile[QPK:], col_n <= step, tile[:QPK])
        top = jnp.max(sc, axis=-1, keepdims=True)
        e = jnp.exp(sc - top)
        nmax[p] = jnp.broadcast_to(top, (QPK, HD))
        nsum[p] = jnp.broadcast_to(jnp.sum(e, axis=-1, keepdims=True), (QPK, HD))
        nacc[p] = dot(e.astype(BF), v)

    arrive(c5, KVH, head)
    col_c = lax.broadcasted_iota(jnp.int32, (qn, ctx), 1)
    col_s = lax.broadcasted_iota(jnp.int32, (qn, 16), 1)
    row_s = lax.broadcasted_iota(jnp.int32, (qn, 16), 0) // QPK

    def cached(r, c):
        load_c(r).wait()
        row = grp * rows + r
        length = jnp.where(rowp[row - quad * qrows] >= 0, 0, clen_ref[row])
        tile = gq[r]
        q = tile[:qn]
        sc = dot_t(q, cache[r, :, :HD]) * scale
        sc = jnp.where(col_c < length, sc, LOW)
        sn, v = fresh(tile[qn:], col_s <= row_s, q)
        top = jnp.maximum(jnp.max(sc, axis=-1, keepdims=True), jnp.max(sn, axis=-1, keepdims=True))
        e = jnp.exp(sc - top)
        en = jnp.exp(sn - top)
        total = jnp.sum(e, axis=-1, keepdims=True) + jnp.sum(en, axis=-1, keepdims=True)
        o = dot(e.astype(BF), cache[r, :, HD:]) + dot(en.astype(BF), v)
        res6[r] = (o / total).astype(BF)
        return c

    lax.fori_loop(0, rows // 2, cached, 0)

    arrive(c2, nslice, mine)
    lane_q = lax.broadcasted_iota(jnp.int32, (qn, HD), 1)
    for h in range(KVH):
        packed = jnp.zeros((qn, HD), F32)
        for i in range(ppd):
            q = q2[h * steps : (h + 1) * steps, i].reshape(qn, HD)
            sc = dot_t(q, keys[i, h]) * scale
            top = jnp.max(sc, axis=-1, keepdims=True)
            e = jnp.exp(sc - top)
            total = jnp.sum(e, axis=-1, keepdims=True)
            v = pkv[i * PAGE : (i + 1) * PAGE, h * 2 * HD + HD : (h + 1) * 2 * HD]
            o = dot(e.astype(BF), v) / total
            stage3[h * steps : (h + 1) * steps, i] = o.astype(BF).reshape(steps, QPK, HD)
            x = jnp.broadcast_to(top + jnp.log(total), (qn, HD))
            packed = jnp.where(lane_q // 3 == i, x, packed)
        hi = packed.astype(BF).astype(F32)
        mid = (packed - hi).astype(BF).astype(F32)
        low = packed - hi - mid
        stat = jnp.where(lane_q % 3 == 0, hi, jnp.where(lane_q % 3 == 1, mid, low))
        stage3[h * steps : (h + 1) * steps, ppd] = stat.astype(BF).reshape(steps, QPK, HD)
    send(c3, nseq, me)
    r3[me] = stage3[mine]

    lax.fori_loop(rows // 2, rows, cached, 0)
    send(c6, KVH, head)
    r6[head] = res6[pl.ds(head * per_src, per_src)]

    arrive(c3, nseq, me)
    pick_r = lax.broadcasted_iota(jnp.int32, (HD, ppd * HD), 0)
    pick_c = lax.broadcasted_iota(jnp.int32, (HD, ppd * HD), 1)
    pick = jnp.where(pick_r // 3 == pick_c // HD, 1.0, 0.0).astype(BF)
    lse[...] = dot(r3[:, ppd].reshape(nseq * QPK, HD), pick)

    def at(g):
        return lse[g // ppd * QPK : (g // ppd + 1) * QPK, g % ppd * HD : (g % ppd + 1) * HD]

    opens = [pfirst[g] == g for g in range(npage)]
    drop = [jnp.where(o, F32(LOW), F32(0.0)) for o in opens]
    keep = [jnp.where(o, F32(0.0), F32(1.0)) for o in opens]
    for g in range(npage):
        run = at(g) if g == 0 else jnp.maximum(at(g), run + drop[g])
        fmax[g] = run
    for g in reversed(range(npage)):
        if g < npage - 1:
            run = jnp.maximum(fmax[g], run + drop[g + 1])
        fmax[g] = run
    for g in range(npage):
        w = jnp.exp(at(g) - fmax[g])
        o = r3[g // ppd, g % ppd].astype(F32) * w
        total = w if g == 0 else w + keep[g] * total
        acc = o if g == 0 else o + keep[g] * acc
        fsum[g] = total
        facc[g] = acc
    for p in range(nprompt):
        g = plast[p]
        top = jnp.maximum(fmax[g], nmax[p])
        a = jnp.exp(fmax[g] - top)
        b = jnp.exp(nmax[p] - top)
        fin[p] = ((facc[g] * a + nacc[p] * b) / (fsum[g] * a + nsum[p] * b)).astype(BF)
    for t in range(nslice):
        for i in range(per_src):
            stage4[t, i] = fin[jnp.maximum(rowp[t * per_src + i], 0)]
    send(c4, nslice, mine)
    r4[mine] = stage4[mine]

    arrive(c6, KVH, head)
    arrive(c4, nslice, mine)
    for i in range(per_src):
        has = rowp[mine * per_src + i]
        chosen = jnp.full((QPK, HD), has, jnp.int32) >= 0
        for h in range(KVH):
            for s in range(steps):
                a = r4[h * steps + s, i].astype(F32)
                b = r6[h, i, s * QPK : (s + 1) * QPK].astype(F32)
                out_ref[i, s, h * QPK : (h + 1) * QPK] = jnp.where(chosen, a, b).astype(BF)

    left(c1, nseq, me)
    left(c2, nslice, mine)
    left(c3, nseq, me)
    left(c4, nslice, mine)
    left(c5, KVH, head)
    left(c6, KVH, head)


def per_device(prompt_kv, prompt_pages, prompt_slot, cache_kv, cache_len, queries, new_kv):
    nseq = lax.axis_size("seq")
    tok_dev = prompt_kv.shape[0]
    ppd = tok_dev // PAGE
    npage = ppd * nseq
    rows, ctx = cache_kv.shape[0], cache_kv.shape[1]
    per_src, steps = queries.shape[0], queries.shape[1]
    nprompt = prompt_pages.shape[0]
    nslice = KVH * steps
    qn = steps * QPK

    q = queries.reshape(per_src, steps, KVH, QPK, HD).transpose(2, 0, 1, 3, 4).reshape(KVH, per_src, qn, HD)
    kv = new_kv.reshape(per_src, steps, KVH, 2, HD).transpose(2, 0, 3, 1, 4).reshape(KVH, per_src, 2 * steps, HD)
    joined = jnp.concatenate([q, kv, jnp.zeros((KVH, per_src, 16 - 2 * steps, HD), BF)], axis=2)
    half = HD // 2
    freq = THETA ** (-(2.0 * jnp.arange(half, dtype=F32)) / HD)
    freq = jnp.broadcast_to(jnp.concatenate([freq, freq])[None], (8, HD))

    smem = pl.BlockSpec(memory_space=pltpu.SMEM)
    vmem = pl.BlockSpec(memory_space=pltpu.VMEM)
    hbm = pl.BlockSpec(memory_space=pl.ANY)
    V = pltpu.VMEM
    D = pltpu.SemaphoreType.DMA
    out = pl.pallas_call(
        functools.partial(kernel, nseq, steps, per_src, ppd, nprompt, ctx),
        out_shape=jax.ShapeDtypeStruct((per_src, steps, KVH * QPK, HD), BF),
        in_specs=[smem, smem, smem, vmem, vmem, hbm, hbm],
        out_specs=vmem,
        scratch_shapes=[
            pltpu.SMEM((npage,), jnp.int32),
            pltpu.SMEM((npage,), jnp.int32),
            pltpu.SMEM((nprompt,), jnp.int32),
            pltpu.SMEM((nslice * per_src,), jnp.int32),
            V((tok_dev, KVH * 2 * HD), BF),
            V((rows, ctx, 2 * HD), BF),
            V((ppd, KVH, PAGE, HD), BF),
            V((nslice, per_src, QPK + 16, HD), BF),
            V((nseq * per_src, QPK + 16, HD), BF),
            V((rows, qn + 16, HD), BF),
            V((nslice, ppd, QPK, HD), BF),
            V((nslice, ppd, QPK, HD), BF),
            V((nslice, ppd + 1, QPK, HD), BF),
            V((nseq, ppd + 1, QPK, HD), BF),
            V((nseq * QPK, ppd * HD), F32),
            V((npage, QPK, HD), F32),
            V((npage, QPK, HD), F32),
            V((npage, QPK, HD), F32),
            V((nprompt, QPK, HD), F32),
            V((nprompt, QPK, HD), F32),
            V((nprompt, QPK, HD), F32),
            V((nprompt, QPK, HD), BF),
            V((nslice, per_src, QPK, HD), BF),
            V((nslice, per_src, QPK, HD), BF),
            V((rows, qn, HD), BF),
            V((KVH, per_src, qn, HD), BF),
            D((rows,)),
            D,
            D((nseq,)), D((nseq,)),
            D((nslice,)), D((nslice,)),
            D((nseq,)), D((nseq,)),
            D((nslice,)), D((nslice,)),
            D((KVH,)), D((KVH,)),
            D((KVH,)), D((KVH,)),
        ],
        compiler_params=pltpu.CompilerParams(
            collective_id=0, has_side_effects=True, vmem_limit_bytes=48 * 1024 * 1024
        ),
    )(prompt_pages, prompt_slot, cache_len, freq, joined, prompt_kv, cache_kv)
    return out.reshape(per_src, steps, KVH * QPK * HD)


def solution(mesh):
    placed = (
        P(("groups", "seq"), None),
        P("groups"),
        P("groups"),
        P(("groups", "seq"), None, None),
        P("groups"),
        P(("groups", "seq"), None, None),
        P(("groups", "seq"), None, None),
    )
    return jax.shard_map(
        per_device,
        mesh=mesh,
        in_specs=placed,
        out_specs=P(("groups", "seq"), None, None),
        check_vma=False,
    )
```

```python
import functools

import jax
import jax.numpy as jnp
from jax import lax
from jax.experimental import pallas as pl
from jax.experimental.pallas import tpu as pltpu
from jax.sharding import PartitionSpec as P

HD = 128
KVH = 4
QPK = 16
PAGE = 128
THETA = 500000.0
LOW = -1e30
MESH = pl.DeviceIdType.MESH
BF = jnp.bfloat16
F32 = jnp.float32


def dot_t(a, b):
    return lax.dot_general(a, b, (((1,), (1,)), ((), ())), preferred_element_type=F32)


def dot(a, b):
    return jnp.dot(a, b, preferred_element_type=F32)


def kernel(
    nseq, steps, per_src, ppd, nprompt, ctx,
    pages_hbm, slot_hbm, clen_hbm, freq_ref, joined_ref, pkv_hbm, cache_hbm,
    out_ref,
    pages_ref, slot_ref, clen_ref, prow, pfirst, plast, rowp,
    pkv, cache, keys, stage1, qall, kvall, gq, stage2, q2, stage3, r3, lse, fmax, fsum, facc,
    nmax, nsum, nacc, fin, stage4, r4, res6, r6,
    csem, psem, isem, s1, t1, s2, t2, s3, t3, s4, t4, s5, t5, s6, t6, s7, t7,
):
    nslice = KVH * steps
    npage = ppd * nseq
    rows = KVH * per_src
    qrows = nslice * per_src
    qn = steps * QPK
    scale = HD ** -0.5
    me = lax.axis_index("seq")
    grp = me // KVH
    head = me % KVH
    quad = me // nslice
    mine = me % nslice
    step = mine % steps
    qbase = quad * nslice

    barrier = pltpu.get_barrier_semaphore()

    def greet(k, c):
        pl.semaphore_signal(barrier, inc=1, device_id={"seq": (me + k) % nseq}, device_id_type=MESH)
        return c

    lax.fori_loop(1, nseq, greet, 0)

    tables = [
        pltpu.make_async_copy(a, b, isem.at[n])
        for n, (a, b) in enumerate([(pages_hbm, pages_ref), (slot_hbm, slot_ref), (clen_hbm, clen_ref)])
    ]
    for table in tables:
        table.start()
    load_p = pltpu.make_async_copy(pkv_hbm, pkv, psem)
    load_p.start()

    def load_c(r):
        return pltpu.make_async_copy(cache_hbm.at[r], cache.at[r], csem.at[r])

    for r in range(rows):
        load_c(r).start()

    for h in range(KVH):
        for s in range(steps):
            for r in range(per_src):
                stage1[h * steps + s, r] = joined_ref[h, r * qn + s * QPK : r * qn + (s + 1) * QPK]

    for table in tables:
        table.wait()

    def page_row(g, c):
        p, start, end = c
        new = g >= end
        p = jnp.minimum(jnp.where(new, p + 1, p), nprompt - 1)
        start = jnp.where(new, end, start)
        end = jnp.where(new, end + pages_ref[p], end)
        prow[g] = slot_ref[p]
        pfirst[g] = start
        return p, start, end

    lax.fori_loop(0, npage, page_row, (jnp.int32(0), jnp.int32(0), pages_ref[0]))

    last = jnp.int32(-1)
    for p in range(nprompt):
        last = last + pages_ref[p]
        plast[p] = jnp.clip(last, 0, npage - 1)

    pl.semaphore_wait(barrier, nseq - 1)

    def c1(t, src):
        return pltpu.make_async_remote_copy(
            src_ref=stage1.at[t % nslice], dst_ref=qall.at[pl.ds(src * per_src, per_src)],
            send_sem=s1.at[t], recv_sem=t1.at[src], device_id={"seq": t}, device_id_type=MESH)

    def c2(t, src):
        return pltpu.make_async_remote_copy(
            src_ref=stage2.at[t], dst_ref=q2.at[src],
            send_sem=s2.at[t], recv_sem=t2.at[src], device_id={"seq": qbase + t}, device_id_type=MESH)

    def c3(t, src):
        return pltpu.make_async_remote_copy(
            src_ref=stage3.at[t % nslice], dst_ref=r3.at[src],
            send_sem=s3.at[t], recv_sem=t3.at[src], device_id={"seq": t}, device_id_type=MESH)

    def c4(t, src):
        return pltpu.make_async_remote_copy(
            src_ref=stage4.at[t], dst_ref=r4.at[src],
            send_sem=s4.at[t], recv_sem=t4.at[src], device_id={"seq": qbase + t}, device_id_type=MESH)

    def c5(t, src):
        return pltpu.make_async_remote_copy(
            src_ref=joined_ref.at[t], dst_ref=gq.at[src],
            send_sem=s5.at[t], recv_sem=t5.at[src], device_id={"seq": grp * KVH + t}, device_id_type=MESH)

    def c6(t, src):
        return pltpu.make_async_remote_copy(
            src_ref=res6.at[pl.ds(t * per_src, per_src)], dst_ref=r6.at[src],
            send_sem=s6.at[t], recv_sem=t6.at[src], device_id={"seq": grp * KVH + t}, device_id_type=MESH)

    def c7(t, src):
        return pltpu.make_async_remote_copy(
            src_ref=joined_ref.at[t % nslice // steps, pl.ds(per_src * qn, 16)], dst_ref=kvall.at[src],
            send_sem=s7.at[t], recv_sem=t7.at[src], device_id={"seq": t}, device_id_type=MESH)

    def send(copy, n, at):
        def go(k, c):
            copy((at + k) % n, at).start()
            return c
        lax.fori_loop(1, n, go, 0)

    def arrive(copy, n, at):
        def go(k, c):
            copy((at + k) % n, (at + n - k) % n).wait_recv()
            return c
        lax.fori_loop(1, n, go, 0)

    def left(copy, n, at):
        def go(k, c):
            copy((at + k) % n, at).wait_send()
            return c
        lax.fori_loop(1, n, go, 0)

    send(c1, nseq, me)
    send(c5, KVH, head)
    qall[pl.ds(me * per_src, per_src)] = stage1[mine]
    gq[head] = joined_ref[head]

    def row_prompt(r, c):
        found = jnp.int32(-1)
        for p in range(nprompt):
            found = jnp.where(slot_ref[p] == r + quad * qrows, p, found)
        rowp[r] = found
        return c

    lax.fori_loop(0, qrows, row_prompt, 0)

    load_p.wait()
    lane = lax.broadcasted_iota(jnp.int32, (PAGE, HD), 1)
    token = lax.broadcasted_iota(jnp.int32, (PAGE, HD), 0)
    for i in range(ppd):
        page = me * ppd + i
        position = (token + (page - pfirst[page]) * PAGE).astype(F32)
        angle = position * freq_ref[0:1, :]
        cosine = jnp.cos(angle)
        sine = jnp.sin(angle)
        sine = jnp.where(lane < HD // 2, -sine, sine)
        for h in range(KVH):
            key = pkv[i * PAGE : (i + 1) * PAGE, h * 2 * HD : h * 2 * HD + HD].astype(F32)
            keys[i, h] = (key * cosine + pltpu.roll(key, HD // 2, 1) * sine).astype(BF)

    arrive(c1, nseq, me)
    for t in range(nslice):
        for i in range(ppd):
            row = prow[(qbase + t) * ppd + i]
            stage2[t, i] = qall[row]
    send(c2, nslice, mine)
    send(c7, nseq, me)
    q2[mine] = stage2[mine]
    kvall[me] = joined_ref[mine // steps, per_src * qn :]

    def fresh(tile, valid, q):
        sc = dot_t(q, tile) * scale
        sc = jnp.where(valid, sc, LOW)
        v = pltpu.roll(tile.astype(F32), 16 - steps, 0).astype(BF)
        return sc, v

    arrive(c5, KVH, head)
    col_c = lax.broadcasted_iota(jnp.int32, (qn, ctx), 1)
    col_s = lax.broadcasted_iota(jnp.int32, (qn, 16), 1)
    row_s = lax.broadcasted_iota(jnp.int32, (qn, 16), 0) // QPK

    def cached(r, c):
        load_c(r).wait()
        row = grp * rows + r
        length = jnp.where(rowp[row - quad * qrows] >= 0, 0, clen_ref[row])
        src, turn = r // per_src, r % per_src
        q = gq[src, pl.ds(pl.multiple_of(turn * qn, qn), qn)]
        sc = dot_t(q, cache[r, :, :HD]) * scale
        sc = jnp.where(col_c < length, sc, LOW)
        place = col_s - turn * 2 * steps
        sn, v = fresh(gq[src, per_src * qn :], (place >= 0) & (place <= row_s), q)
        top = jnp.maximum(jnp.max(sc, axis=-1, keepdims=True), jnp.max(sn, axis=-1, keepdims=True))
        e = jnp.exp(sc - top)
        en = jnp.exp(sn - top)
        total = jnp.sum(e, axis=-1, keepdims=True) + jnp.sum(en, axis=-1, keepdims=True)
        o = dot(e.astype(BF), cache[r, :, HD:]) + dot(en.astype(BF), v)
        res6[r] = (o / total).astype(BF)
        return c

    lax.fori_loop(0, rows // 2, cached, 0)

    lane_q = lax.broadcasted_iota(jnp.int32, (qn, HD), 1)
    for h in range(KVH):
        for s in range(steps):
            @pl.when(h * steps + s != mine)
            def _():
                c2(mine, h * steps + s).wait_recv()
        packed = jnp.zeros((qn, HD), F32)
        for i in range(ppd):
            q = q2[h * steps : (h + 1) * steps, i].reshape(qn, HD)
            sc = dot_t(q, keys[i, h]) * scale
            top = jnp.max(sc, axis=-1, keepdims=True)
            e = jnp.exp(sc - top)
            total = jnp.sum(e, axis=-1, keepdims=True)
            v = pkv[i * PAGE : (i + 1) * PAGE, h * 2 * HD + HD : (h + 1) * 2 * HD]
            o = dot(e.astype(BF), v) / total
            stage3[h * steps : (h + 1) * steps, i] = o.astype(BF).reshape(steps, QPK, HD)
            x = jnp.broadcast_to(top + jnp.log(total), (qn, HD))
            packed = jnp.where(lane_q // 3 == i, x, packed)
        hi = packed.astype(BF).astype(F32)
        mid = (packed - hi).astype(BF).astype(F32)
        low = packed - hi - mid
        stat = jnp.where(lane_q % 3 == 0, hi, jnp.where(lane_q % 3 == 1, mid, low))
        stage3[h * steps : (h + 1) * steps, ppd] = stat.astype(BF).reshape(steps, QPK, HD)
        for block in range(nseq // nslice):
            for s in range(steps):
                t = block * nslice + h * steps + s
                @pl.when(t != me)
                def _():
                    c3(t, me).start()
    r3[me] = stage3[mine]

    arrive(c7, nseq, me)
    col_n = lax.broadcasted_iota(jnp.int32, (QPK, 16), 1)
    for p in range(nprompt):
        row = slot_ref[p]
        place = col_n - row % per_src * 2 * steps
        sc, v = fresh(kvall[row // per_src], (place >= 0) & (place <= step), qall[row])
        top = jnp.max(sc, axis=-1, keepdims=True)
        e = jnp.exp(sc - top)
        nmax[p] = jnp.broadcast_to(top, (QPK, HD))
        nsum[p] = jnp.broadcast_to(jnp.sum(e, axis=-1, keepdims=True), (QPK, HD))
        nacc[p] = dot(e.astype(BF), v)

    lax.fori_loop(rows // 2, rows, cached, 0)
    send(c6, KVH, head)
    r6[head] = res6[pl.ds(head * per_src, per_src)]

    arrive(c3, nseq, me)
    pick_r = lax.broadcasted_iota(jnp.int32, (HD, ppd * HD), 0)
    pick_c = lax.broadcasted_iota(jnp.int32, (HD, ppd * HD), 1)
    pick = jnp.where(pick_r // 3 == pick_c // HD, 1.0, 0.0).astype(BF)
    lse[...] = dot(r3[:, ppd].reshape(nseq * QPK, HD), pick)

    def at(g):
        return lse[g // ppd * QPK : (g // ppd + 1) * QPK, g % ppd * HD : (g % ppd + 1) * HD]

    opens = [pfirst[g] == g for g in range(npage)]
    drop = [jnp.where(o, F32(LOW), F32(0.0)) for o in opens]
    keep = [jnp.where(o, F32(0.0), F32(1.0)) for o in opens]
    for g in range(npage):
        run = at(g) if g == 0 else jnp.maximum(at(g), run + drop[g])
        fmax[g] = run
    for g in reversed(range(npage)):
        if g < npage - 1:
            run = jnp.maximum(fmax[g], run + drop[g + 1])
        fmax[g] = run
    for g in range(npage):
        w = jnp.exp(at(g) - fmax[g])
        o = r3[g // ppd, g % ppd].astype(F32) * w
        total = w if g == 0 else w + keep[g] * total
        acc = o if g == 0 else o + keep[g] * acc
        fsum[g] = total
        facc[g] = acc
    for p in range(nprompt):
        g = plast[p]
        top = jnp.maximum(fmax[g], nmax[p])
        a = jnp.exp(fmax[g] - top)
        b = jnp.exp(nmax[p] - top)
        fin[p] = ((facc[g] * a + nacc[p] * b) / (fsum[g] * a + nsum[p] * b)).astype(BF)
    for t in range(nslice):
        for i in range(per_src):
            stage4[t, i] = fin[jnp.maximum(rowp[t * per_src + i], 0)]
    send(c4, nslice, mine)
    r4[mine] = stage4[mine]

    arrive(c6, KVH, head)
    arrive(c4, nslice, mine)
    for i in range(per_src):
        has = rowp[mine * per_src + i]
        chosen = jnp.full((QPK, HD), has, jnp.int32) >= 0
        for h in range(KVH):
            for s in range(steps):
                a = r4[h * steps + s, i].astype(F32)
                b = r6[h, i, s * QPK : (s + 1) * QPK].astype(F32)
                out_ref[i, s, h * QPK : (h + 1) * QPK] = jnp.where(chosen, a, b).astype(BF)

    left(c1, nseq, me)
    left(c2, nslice, mine)
    left(c3, nseq, me)
    left(c4, nslice, mine)
    left(c5, KVH, head)
    left(c6, KVH, head)
    left(c7, nseq, me)


def per_device(prompt_kv, prompt_pages, prompt_slot, cache_kv, cache_len, queries, new_kv):
    nseq = lax.axis_size("seq")
    tok_dev = prompt_kv.shape[0]
    ppd = tok_dev // PAGE
    npage = ppd * nseq
    rows, ctx = cache_kv.shape[0], cache_kv.shape[1]
    per_src, steps = queries.shape[0], queries.shape[1]
    nprompt = prompt_pages.shape[0]
    nslice = KVH * steps
    qn = steps * QPK

    q = queries.reshape(per_src, steps, KVH, QPK, HD).transpose(2, 0, 1, 3, 4).reshape(KVH, per_src * qn, HD)
    kv = new_kv.reshape(per_src, steps, KVH, 2, HD).transpose(2, 0, 3, 1, 4).reshape(KVH, per_src * 2 * steps, HD)
    joined = jnp.concatenate([q, kv], axis=1)
    half = HD // 2
    freq = THETA ** (-(2.0 * jnp.arange(half, dtype=F32)) / HD)
    freq = jnp.broadcast_to(jnp.concatenate([freq, freq])[None], (8, HD))

    vmem = pl.BlockSpec(memory_space=pltpu.VMEM)
    hbm = pl.BlockSpec(memory_space=pl.ANY)
    V = pltpu.VMEM
    D = pltpu.SemaphoreType.DMA
    out = pl.pallas_call(
        functools.partial(kernel, nseq, steps, per_src, ppd, nprompt, ctx),
        out_shape=jax.ShapeDtypeStruct((per_src, steps, KVH * QPK, HD), BF),
        in_specs=[hbm, hbm, hbm, vmem, vmem, hbm, hbm],
        out_specs=vmem,
        scratch_shapes=[
            pltpu.SMEM(prompt_pages.shape, jnp.int32),
            pltpu.SMEM(prompt_slot.shape, jnp.int32),
            pltpu.SMEM(cache_len.shape, jnp.int32),
            pltpu.SMEM((npage,), jnp.int32),
            pltpu.SMEM((npage,), jnp.int32),
            pltpu.SMEM((nprompt,), jnp.int32),
            pltpu.SMEM((nslice * per_src,), jnp.int32),
            V((tok_dev, KVH * 2 * HD), BF),
            V((rows, ctx, 2 * HD), BF),
            V((ppd, KVH, PAGE, HD), BF),
            V((nslice, per_src, QPK, HD), BF),
            V((nseq * per_src, QPK, HD), BF),
            V((nseq, 16, HD), BF),
            V((KVH, per_src * qn + 16, HD), BF),
            V((nslice, ppd, QPK, HD), BF),
            V((nslice, ppd, QPK, HD), BF),
            V((nslice, ppd + 1, QPK, HD), BF),
            V((nseq, ppd + 1, QPK, HD), BF),
            V((nseq * QPK, ppd * HD), F32),
            V((npage, QPK, HD), F32),
            V((npage, QPK, HD), F32),
            V((npage, QPK, HD), F32),
            V((nprompt, QPK, HD), F32),
            V((nprompt, QPK, HD), F32),
            V((nprompt, QPK, HD), F32),
            V((nprompt, QPK, HD), BF),
            V((nslice, per_src, QPK, HD), BF),
            V((nslice, per_src, QPK, HD), BF),
            V((rows, qn, HD), BF),
            V((KVH, per_src, qn, HD), BF),
            D((rows,)),
            D,
            D((3,)),
            D((nseq,)), D((nseq,)),
            D((nslice,)), D((nslice,)),
            D((nseq,)), D((nseq,)),
            D((nslice,)), D((nslice,)),
            D((KVH,)), D((KVH,)),
            D((KVH,)), D((KVH,)),
            D((nseq,)), D((nseq,)),
        ],
        compiler_params=pltpu.CompilerParams(
            collective_id=0, has_side_effects=True, vmem_limit_bytes=62 * 1024 * 1024
        ),
    )(prompt_pages, prompt_slot, cache_len, freq, joined, prompt_kv, cache_kv)
    return out.reshape(per_src, steps, KVH * QPK * HD)


def solution(mesh):
    placed = (
        P(("groups", "seq"), None),
        P("groups"),
        P("groups"),
        P(("groups", "seq"), None, None),
        P("groups"),
        P(("groups", "seq"), None, None),
        P(("groups", "seq"), None, None),
    )
    return jax.shard_map(
        per_device,
        mesh=mesh,
        in_specs=placed,
        out_specs=P(("groups", "seq"), None, None),
        check_vma=False,
    )
```

```python
import functools
import math

import jax
import jax.numpy as jnp
from jax import lax
from jax.experimental import pallas as pl
from jax.experimental.pallas import tpu as pltpu
from jax.sharding import PartitionSpec as P

HD = 128
KVH = 4
QPK = 16
PAGE = 128
THETA = 500000.0
LOW = -1e30
MESH = pl.DeviceIdType.MESH
BF = jnp.bfloat16
F32 = jnp.float32


def dot_t(a, b):
    return lax.dot_general(a, b, (((1,), (1,)), ((), ())), preferred_element_type=F32)


def dot(a, b):
    return jnp.dot(a, b, preferred_element_type=F32)


def kernel(
    nseq, steps, per_src, ppd, nprompt, ctx,
    pages_hbm, slot_hbm, clen_hbm, q_hbm, kv_hbm, pkv_hbm, cache_hbm,
    out_ref,
    pages_ref, slot_ref, clen_ref, prow, pfirst, plast, rowp,
    qin, kvin, kvf, joined_ref, pkv, cache, keys, stage1, qall, kvall, gq, stage2, q2, stage3, r3, lse, fmax, fsum, facc,
    nmax, nsum, nacc, fin, stage4, r4, res6, r6,
    csem, psem, isem, s1, t1, s2, t2, s3, t3, s4, t4, s5, t5, s6, t6, s7, t7,
):
    nslice = KVH * steps
    npage = ppd * nseq
    rows = KVH * per_src
    qrows = nslice * per_src
    qn = steps * QPK
    scale = HD ** -0.5
    me = lax.axis_index("seq")
    grp = me // KVH
    head = me % KVH
    quad = me // nslice
    mine = me % nslice
    step = mine % steps
    qbase = quad * nslice

    barrier = pltpu.get_barrier_semaphore()

    def far_first(n):
        return sorted(range(1, n), key=lambda k: abs(2 * k - n))

    def wrap(t, n):
        return jnp.where(t >= n, t - n, t)

    def piece(t):
        return t if nseq == nslice else t % nslice

    for k in far_first(nseq):
        pl.semaphore_signal(barrier, inc=1, device_id={"seq": wrap(me + k, nseq)}, device_id_type=MESH)

    tables = [
        pltpu.make_async_copy(a, b, isem.at[n])
        for n, (a, b) in enumerate([(pages_hbm, pages_ref), (slot_hbm, slot_ref), (clen_hbm, clen_ref), (q_hbm, qin), (kv_hbm, kvin)])
    ]
    for table in tables:
        table.start()
    def load_c(r):
        return pltpu.make_async_copy(cache_hbm.at[r], cache.at[r], csem.at[r])

    load_p = pltpu.make_async_copy(pkv_hbm, pkv, psem)
    load_p.start()
    for r in range(rows):
        load_c(r).start()
    tables[3].wait()
    for r in range(per_src):
        x = qin[r].astype(F32).reshape(steps, KVH * QPK, HD)
        for h in range(KVH):
            for s in range(steps):
                tile = x[s, h * QPK : (h + 1) * QPK].astype(BF)
                stage1[h * steps + s, r] = tile
                joined_ref[h, r * qn + s * QPK : r * qn + (s + 1) * QPK] = tile

    pl.semaphore_wait(barrier, nseq - 1)

    def c1(t, src):
        return pltpu.make_async_remote_copy(
            src_ref=stage1.at[piece(t)], dst_ref=qall.at[pl.ds(src * per_src, per_src)],
            send_sem=s1.at[t], recv_sem=t1.at[src], device_id={"seq": t}, device_id_type=MESH)

    def c2(t, src):
        return pltpu.make_async_remote_copy(
            src_ref=stage2.at[t], dst_ref=q2.at[src],
            send_sem=s2.at[t], recv_sem=t2.at[src], device_id={"seq": qbase + t}, device_id_type=MESH)

    def c3(t, src):
        return pltpu.make_async_remote_copy(
            src_ref=stage3.at[piece(t)], dst_ref=r3.at[src],
            send_sem=s3.at[t], recv_sem=t3.at[src], device_id={"seq": t}, device_id_type=MESH)

    def c4(t, src):
        return pltpu.make_async_remote_copy(
            src_ref=stage4.at[t], dst_ref=r4.at[src],
            send_sem=s4.at[t], recv_sem=t4.at[src], device_id={"seq": qbase + t}, device_id_type=MESH)

    def c5(t, src):
        return pltpu.make_async_remote_copy(
            src_ref=joined_ref.at[t], dst_ref=gq.at[src],
            send_sem=s5.at[t], recv_sem=t5.at[src], device_id={"seq": grp * KVH + t}, device_id_type=MESH)

    def c6(t, src):
        return pltpu.make_async_remote_copy(
            src_ref=res6.at[pl.ds(t * per_src, per_src)], dst_ref=r6.at[src],
            send_sem=s6.at[t], recv_sem=t6.at[src], device_id={"seq": grp * KVH + t}, device_id_type=MESH)

    def c7(t, src):
        return pltpu.make_async_remote_copy(
            src_ref=joined_ref.at[piece(t) // steps, pl.ds(per_src * qn, 16)], dst_ref=kvall.at[src],
            send_sem=s7.at[t], recv_sem=t7.at[src], device_id={"seq": t}, device_id_type=MESH)

    def send(copy, n, at):
        for k in far_first(n):
            copy(wrap(at + k, n), at).start()

    def arrive(copy, n, at):
        for k in reversed(far_first(n)):
            copy(wrap(at + k, n), wrap(at + n - k, n)).wait_recv()

    def left(copy, n, at):
        for k in far_first(n):
            copy(wrap(at + k, n), at).wait_send()

    send(c1, nseq, me)
    for n in (4, 0, 1, 2):
        tables[n].wait()
    for r in range(per_src):
        x = kvin[r].astype(F32)
        for h in range(KVH):
            for part in range(2):
                at = (r * 2 + part) * steps
                kvf[h, at : at + steps] = x[:, (h * 2 + part) * HD : (h * 2 + part + 1) * HD]
    joined_ref[:, per_src * qn :] = kvf[...].astype(BF)
    send(c5, KVH, head)
    qall[pl.ds(me * per_src, per_src)] = stage1[mine]
    gq[head] = joined_ref[head]

    def page_row(g, c):
        p, start, end = c
        new = g >= end
        p = jnp.minimum(jnp.where(new, p + 1, p), nprompt - 1)
        start = jnp.where(new, end, start)
        end = jnp.where(new, end + pages_ref[p], end)
        prow[g] = slot_ref[p]
        pfirst[g] = start
        return p, start, end

    lax.fori_loop(0, npage, page_row, (jnp.int32(0), jnp.int32(0), pages_ref[0]))

    last = jnp.int32(-1)
    for p in range(nprompt):
        last = last + pages_ref[p]
        plast[p] = jnp.clip(last, 0, npage - 1)

    def row_prompt(r, c):
        found = jnp.int32(-1)
        for p in range(nprompt):
            found = jnp.where(slot_ref[p] == r + quad * qrows, p, found)
        rowp[r] = found
        return c

    lax.fori_loop(0, qrows, row_prompt, 0)

    load_p.wait()
    lane = lax.broadcasted_iota(jnp.int32, (PAGE, HD), 1)
    freq = jnp.exp((lane % (HD // 2)).astype(F32) * (-2.0 * math.log(THETA) / HD))
    token = lax.broadcasted_iota(jnp.int32, (PAGE, HD), 0)
    for i in range(ppd):
        page = me * ppd + i
        position = (token + (page - pfirst[page]) * PAGE).astype(F32)
        angle = position * freq
        cosine = jnp.cos(angle)
        sine = jnp.sin(angle)
        sine = jnp.where(lane < HD // 2, -sine, sine)
        for h in range(KVH):
            key = pkv[i * PAGE : (i + 1) * PAGE, h * 2 * HD : h * 2 * HD + HD].astype(F32)
            keys[i, h] = (key * cosine + pltpu.roll(key, HD // 2, 1) * sine).astype(BF)

    send(c7, nseq, me)

    arrive(c1, nseq, me)
    for t in range(nslice):
        for i in range(ppd):
            row = prow[(qbase + t) * ppd + i]
            stage2[t, i] = qall[row]
    send(c2, nslice, mine)
    q2[mine] = stage2[mine]
    kvall[me] = joined_ref[mine // steps, per_src * qn :]

    def fresh(tile, valid, q):
        sc = dot_t(q, tile) * scale
        sc = jnp.where(valid, sc, LOW)
        v = pltpu.roll(tile.astype(F32), 16 - steps, 0).astype(BF)
        return sc, v

    arrive(c5, KVH, head)
    col_c = lax.broadcasted_iota(jnp.int32, (qn, ctx), 1)
    col_s = lax.broadcasted_iota(jnp.int32, (qn, 16), 1)
    row_s = lax.broadcasted_iota(jnp.int32, (qn, 16), 0) // QPK

    def cached(r, c):
        load_c(r).wait()
        row = grp * rows + r
        length = jnp.where(rowp[row - quad * qrows] >= 0, 0, clen_ref[row])
        src, turn = r // per_src, r % per_src
        q = gq[src, pl.ds(pl.multiple_of(turn * qn, qn), qn)]
        sc = dot_t(q, cache[r, :, :HD]) * scale
        sc = jnp.where(col_c < length, sc, LOW)
        place = col_s - turn * 2 * steps
        sn, v = fresh(gq[src, per_src * qn :], (place >= 0) & (place <= row_s), q)
        top = jnp.maximum(jnp.max(sc, axis=-1, keepdims=True), jnp.max(sn, axis=-1, keepdims=True))
        e = jnp.exp(sc - top)
        en = jnp.exp(sn - top)
        total = jnp.sum(e, axis=-1, keepdims=True) + jnp.sum(en, axis=-1, keepdims=True)
        o = dot(e.astype(BF), cache[r, :, HD:]) + dot(en.astype(BF), v)
        res6[r] = (o / total).astype(BF)
        return c

    lax.fori_loop(0, rows // 2, cached, 0)

    lane_q = lax.broadcasted_iota(jnp.int32, (qn, HD), 1)
    def pages_of(h):
        for s in range(steps):
            @pl.when(h * steps + s != mine)
            def _():
                c2(mine, h * steps + s).wait_recv()
        packed = jnp.zeros((qn, HD), F32)
        for i in range(ppd):
            q = q2[h * steps : (h + 1) * steps, i].reshape(qn, HD)
            sc = dot_t(q, keys[i, h]) * scale
            top = jnp.max(sc, axis=-1, keepdims=True)
            e = jnp.exp(sc - top)
            total = jnp.sum(e, axis=-1, keepdims=True)
            v = pkv[i * PAGE : (i + 1) * PAGE, h * 2 * HD + HD : (h + 1) * 2 * HD]
            o = dot(e.astype(BF), v) / total
            stage3[h * steps : (h + 1) * steps, i] = o.astype(BF).reshape(steps, QPK, HD)
            x = jnp.broadcast_to(top + jnp.log(total), (qn, HD))
            packed = jnp.where(lane_q // 3 == i, x, packed)
        hi = packed.astype(BF).astype(F32)
        mid = (packed - hi).astype(BF).astype(F32)
        low = packed - hi - mid
        stat = jnp.where(lane_q % 3 == 0, hi, jnp.where(lane_q % 3 == 1, mid, low))
        stage3[h * steps : (h + 1) * steps, ppd] = stat.astype(BF).reshape(steps, QPK, HD)
        for block in range(nseq // nslice):
            for s in range(steps):
                t = block * nslice + h * steps + s
                @pl.when(t != me)
                def _():
                    c3(t, me).start()
    for plane in range(KVH):
        @pl.when(mine // steps == plane)
        def _():
            for k in (2, 1, 3, 0):
                pages_of((plane + k) % KVH)

    r3[me] = stage3[mine]

    arrive(c7, nseq, me)
    col_n = lax.broadcasted_iota(jnp.int32, (QPK, 16), 1)
    for p in range(nprompt):
        row = slot_ref[p]
        place = col_n - row % per_src * 2 * steps
        sc, v = fresh(kvall[row // per_src], (place >= 0) & (place <= step), qall[row])
        top = jnp.max(sc, axis=-1, keepdims=True)
        e = jnp.exp(sc - top)
        nmax[p] = jnp.broadcast_to(top, (QPK, HD))
        nsum[p] = jnp.broadcast_to(jnp.sum(e, axis=-1, keepdims=True), (QPK, HD))
        nacc[p] = dot(e.astype(BF), v)

    lax.fori_loop(rows // 2, rows, cached, 0)
    send(c6, KVH, head)
    r6[head] = res6[pl.ds(head * per_src, per_src)]

    arrive(c3, nseq, me)
    pick_r = lax.broadcasted_iota(jnp.int32, (HD, ppd * HD), 0)
    pick_c = lax.broadcasted_iota(jnp.int32, (HD, ppd * HD), 1)
    pick = jnp.where(pick_r // 3 == pick_c // HD, 1.0, 0.0).astype(BF)
    lse[...] = dot(r3[:, ppd].reshape(nseq * QPK, HD), pick)

    def at(g):
        return lse[g // ppd * QPK : (g // ppd + 1) * QPK, g % ppd * HD : (g % ppd + 1) * HD]

    opens = [pfirst[g] == g for g in range(npage)]
    drop = [jnp.where(o, F32(LOW), F32(0.0)) for o in opens]
    keep = [jnp.where(o, F32(0.0), F32(1.0)) for o in opens]
    for g in range(npage):
        run = at(g) if g == 0 else jnp.maximum(at(g), run + drop[g])
        fmax[g] = run
    for g in reversed(range(npage)):
        if g < npage - 1:
            run = jnp.maximum(fmax[g], run + drop[g + 1])
        fmax[g] = run
    for g in range(npage):
        w = jnp.exp(at(g) - fmax[g])
        o = r3[g // ppd, g % ppd].astype(F32) * w
        total = w if g == 0 else w + keep[g] * total
        acc = o if g == 0 else o + keep[g] * acc
        fsum[g] = total
        facc[g] = acc
    for p in range(nprompt):
        g = plast[p]
        top = jnp.maximum(fmax[g], nmax[p])
        a = jnp.exp(fmax[g] - top)
        b = jnp.exp(nmax[p] - top)
        fin[p] = ((facc[g] * a + nacc[p] * b) / (fsum[g] * a + nsum[p] * b)).astype(BF)
    for t in range(nslice):
        for i in range(per_src):
            stage4[t, i] = fin[jnp.maximum(rowp[t * per_src + i], 0)]
    send(c4, nslice, mine)
    r4[mine] = stage4[mine]

    arrive(c6, KVH, head)
    arrive(c4, nslice, mine)
    for i in range(per_src):
        has = rowp[mine * per_src + i]
        chosen = jnp.full((QPK, HD), has, jnp.int32) >= 0
        for h in range(KVH):
            for s in range(steps):
                a = r4[h * steps + s, i].astype(F32)
                b = r6[h, i, s * QPK : (s + 1) * QPK].astype(F32)
                out_ref[i, s, h * QPK : (h + 1) * QPK] = jnp.where(chosen, a, b).astype(BF)

    left(c1, nseq, me)
    left(c2, nslice, mine)
    left(c3, nseq, me)
    left(c4, nslice, mine)
    left(c5, KVH, head)
    left(c6, KVH, head)
    left(c7, nseq, me)


def per_device(prompt_kv, prompt_pages, prompt_slot, cache_kv, cache_len, queries, new_kv):
    nseq = lax.axis_size("seq")
    tok_dev = prompt_kv.shape[0]
    ppd = tok_dev // PAGE
    npage = ppd * nseq
    rows, ctx = cache_kv.shape[0], cache_kv.shape[1]
    per_src, steps = queries.shape[0], queries.shape[1]
    nprompt = prompt_pages.shape[0]
    nslice = KVH * steps
    qn = steps * QPK

    vmem = pl.BlockSpec(memory_space=pltpu.VMEM)
    hbm = pl.BlockSpec(memory_space=pl.ANY)
    V = pltpu.VMEM
    D = pltpu.SemaphoreType.DMA
    out = pl.pallas_call(
        functools.partial(kernel, nseq, steps, per_src, ppd, nprompt, ctx),
        out_shape=jax.ShapeDtypeStruct((per_src, steps, KVH * QPK, HD), BF),
        in_specs=[hbm] * 7,
        out_specs=vmem,
        scratch_shapes=[
            pltpu.SMEM(prompt_pages.shape, jnp.int32),
            pltpu.SMEM(prompt_slot.shape, jnp.int32),
            pltpu.SMEM(cache_len.shape, jnp.int32),
            pltpu.SMEM((npage,), jnp.int32),
            pltpu.SMEM((npage,), jnp.int32),
            pltpu.SMEM((nprompt,), jnp.int32),
            pltpu.SMEM((nslice * per_src,), jnp.int32),
            V(queries.shape, BF),
            V(new_kv.shape, BF),
            V((KVH, 16, HD), F32),
            V((KVH, per_src * qn + 16, HD), BF),
            V((tok_dev, KVH * 2 * HD), BF),
            V((rows, ctx, 2 * HD), BF),
            V((ppd, KVH, PAGE, HD), BF),
            V((nslice, per_src, QPK, HD), BF),
            V((nseq * per_src, QPK, HD), BF),
            V((nseq, 16, HD), BF),
            V((KVH, per_src * qn + 16, HD), BF),
            V((nslice, ppd, QPK, HD), BF),
            V((nslice, ppd, QPK, HD), BF),
            V((nslice, ppd + 1, QPK, HD), BF),
            V((nseq, ppd + 1, QPK, HD), BF),
            V((nseq * QPK, ppd * HD), F32),
            V((npage, QPK, HD), F32),
            V((npage, QPK, HD), F32),
            V((npage, QPK, HD), F32),
            V((nprompt, QPK, HD), F32),
            V((nprompt, QPK, HD), F32),
            V((nprompt, QPK, HD), F32),
            V((nprompt, QPK, HD), BF),
            V((nslice, per_src, QPK, HD), BF),
            V((nslice, per_src, QPK, HD), BF),
            V((rows, qn, HD), BF),
            V((KVH, per_src, qn, HD), BF),
            D((rows,)),
            D,
            D((5,)),
            D((nseq,)), D((nseq,)),
            D((nslice,)), D((nslice,)),
            D((nseq,)), D((nseq,)),
            D((nslice,)), D((nslice,)),
            D((KVH,)), D((KVH,)),
            D((KVH,)), D((KVH,)),
            D((nseq,)), D((nseq,)),
        ],
        compiler_params=pltpu.CompilerParams(
            collective_id=0, has_side_effects=True, vmem_limit_bytes=62 * 1024 * 1024
        ),
    )(prompt_pages, prompt_slot, cache_len, queries, new_kv, prompt_kv, cache_kv)
    return out.reshape(per_src, steps, KVH * QPK * HD)


def solution(mesh):
    placed = (
        P(("groups", "seq"), None),
        P("groups"),
        P("groups"),
        P(("groups", "seq"), None, None),
        P("groups"),
        P(("groups", "seq"), None, None),
        P(("groups", "seq"), None, None),
    )
    return jax.shard_map(
        per_device,
        mesh=mesh,
        in_specs=placed,
        out_specs=P(("groups", "seq"), None, None),
        check_vma=False,
    )
```

```python
import functools
import math

import jax
import jax.numpy as jnp
from jax import lax
from jax.experimental import pallas as pl
from jax.experimental.pallas import tpu as pltpu
from jax.sharding import PartitionSpec as P

HD = 128
KVH = 4
QPK = 16
PAGE = 128
THETA = 500000.0
LOW = -1e30
MESH = pl.DeviceIdType.MESH
BF = jnp.bfloat16
F32 = jnp.float32


def dot_t(a, b):
    return lax.dot_general(a, b, (((1,), (1,)), ((), ())), preferred_element_type=F32)


def dot(a, b):
    return jnp.dot(a, b, preferred_element_type=F32)


def kernel(
    nseq, steps, per_src, ppd, nprompt, ctx,
    pages_hbm, slot_hbm, clen_hbm, q_hbm, kv_hbm, pkv_hbm, cache_hbm,
    out_ref,
    pages_ref, slot_ref, clen_ref, prow, pfirst, plast, rowp,
    qin, kvin, kvf, joined_ref, pkv, cache, keys, stage1, qall, kvall, gq, stage2, q2, stage3, r3, lse, fmax, fsum, facc,
    nmax, nsum, nacc, fin, stage4, r4, res6, r6,
    csem, psem, isem, s1, t1, s2, t2, s3, t3, s4, t4, s5, t5, s6, t6, s7, t7,
):
    nslice = KVH * steps
    npage = ppd * nseq
    rows = KVH * per_src
    qrows = nslice * per_src
    qn = steps * QPK
    scale = HD ** -0.5
    me = lax.axis_index("seq")
    grp = me // KVH
    head = me % KVH
    quad = me // nslice
    mine = me % nslice
    step = mine % steps
    qbase = quad * nslice

    barrier = pltpu.get_barrier_semaphore()

    def partners(n):
        return list(range(1, n))

    def wrap(t, n):
        return jnp.where(t >= n, t - n, t)

    def piece(t):
        return t if nseq == nslice else t % nslice

    for k in partners(nseq):
        pl.semaphore_signal(barrier, inc=1, device_id={"seq": wrap(me + k, nseq)}, device_id_type=MESH)

    tables = [
        pltpu.make_async_copy(a, b, isem.at[n])
        for n, (a, b) in enumerate([(pages_hbm, pages_ref), (slot_hbm, slot_ref), (clen_hbm, clen_ref), (q_hbm, qin), (kv_hbm, kvin)])
    ]
    for table in tables:
        table.start()
    def load_c(r):
        return pltpu.make_async_copy(cache_hbm.at[r], cache.at[r], csem.at[r])

    load_p = pltpu.make_async_copy(pkv_hbm, pkv, psem)
    load_p.start()
    for r in range(rows):
        load_c(r).start()
    tables[3].wait()
    for r in range(per_src):
        x = qin[r].astype(F32).reshape(steps, KVH * QPK, HD)
        for h in range(KVH):
            for s in range(steps):
                tile = x[s, h * QPK : (h + 1) * QPK].astype(BF)
                stage1[h * steps + s, r] = tile
                joined_ref[h, r * qn + s * QPK : r * qn + (s + 1) * QPK] = tile

    pl.semaphore_wait(barrier, nseq - 1)

    def c1(t, src):
        return pltpu.make_async_remote_copy(
            src_ref=stage1.at[piece(t)], dst_ref=qall.at[pl.ds(src * per_src, per_src)],
            send_sem=s1.at[t], recv_sem=t1.at[src], device_id={"seq": t}, device_id_type=MESH)

    def c2(t, src):
        return pltpu.make_async_remote_copy(
            src_ref=stage2.at[t], dst_ref=q2.at[src],
            send_sem=s2.at[t], recv_sem=t2.at[src], device_id={"seq": qbase + t}, device_id_type=MESH)

    def c3(t, src):
        return pltpu.make_async_remote_copy(
            src_ref=stage3.at[piece(t)], dst_ref=r3.at[src],
            send_sem=s3.at[t], recv_sem=t3.at[src], device_id={"seq": t}, device_id_type=MESH)

    def c4(t, src):
        return pltpu.make_async_remote_copy(
            src_ref=stage4.at[t], dst_ref=r4.at[src],
            send_sem=s4.at[t], recv_sem=t4.at[src], device_id={"seq": qbase + t}, device_id_type=MESH)

    def c5(t, src):
        return pltpu.make_async_remote_copy(
            src_ref=joined_ref.at[t], dst_ref=gq.at[src],
            send_sem=s5.at[t], recv_sem=t5.at[src], device_id={"seq": grp * KVH + t}, device_id_type=MESH)

    def c6(t, src):
        return pltpu.make_async_remote_copy(
            src_ref=res6.at[pl.ds(t * per_src, per_src)], dst_ref=r6.at[src],
            send_sem=s6.at[t], recv_sem=t6.at[src], device_id={"seq": grp * KVH + t}, device_id_type=MESH)

    def c7(t, src):
        return pltpu.make_async_remote_copy(
            src_ref=joined_ref.at[piece(t) // steps, pl.ds(per_src * qn, 16)], dst_ref=kvall.at[src],
            send_sem=s7.at[t], recv_sem=t7.at[src], device_id={"seq": t}, device_id_type=MESH)

    def send(copy, n, at):
        for k in partners(n):
            copy(wrap(at + k, n), at).start()

    def arrive(copy, n, at):
        for k in reversed(partners(n)):
            copy(wrap(at + k, n), wrap(at + n - k, n)).wait_recv()

    def left(copy, n, at):
        for k in partners(n):
            copy(wrap(at + k, n), at).wait_send()

    send(c1, nseq, me)
    for n in (4, 0, 1, 2):
        tables[n].wait()
    for r in range(per_src):
        x = kvin[r].astype(F32)
        for h in range(KVH):
            for part in range(2):
                at = (r * 2 + part) * steps
                kvf[h, at : at + steps] = x[:, (h * 2 + part) * HD : (h * 2 + part + 1) * HD]
    joined_ref[:, per_src * qn :] = kvf[...].astype(BF)
    send(c5, KVH, head)
    qall[pl.ds(me * per_src, per_src)] = stage1[mine]
    gq[head] = joined_ref[head]

    def page_row(g, c):
        p, start, end = c
        new = g >= end
        p = jnp.minimum(jnp.where(new, p + 1, p), nprompt - 1)
        start = jnp.where(new, end, start)
        end = jnp.where(new, end + pages_ref[p], end)
        prow[g] = slot_ref[p]
        pfirst[g] = start
        return p, start, end

    lax.fori_loop(0, npage, page_row, (jnp.int32(0), jnp.int32(0), pages_ref[0]))

    last = jnp.int32(-1)
    for p in range(nprompt):
        last = last + pages_ref[p]
        plast[p] = jnp.clip(last, 0, npage - 1)

    def row_prompt(r, c):
        found = jnp.int32(-1)
        for p in range(nprompt):
            found = jnp.where(slot_ref[p] == r + quad * qrows, p, found)
        rowp[r] = found
        return c

    lax.fori_loop(0, qrows, row_prompt, 0)

    load_p.wait()
    lane = lax.broadcasted_iota(jnp.int32, (PAGE, HD), 1)
    freq = jnp.exp((lane % (HD // 2)).astype(F32) * (-2.0 * math.log(THETA) / HD))
    token = lax.broadcasted_iota(jnp.int32, (PAGE, HD), 0)
    for i in range(ppd):
        page = me * ppd + i
        position = (token + (page - pfirst[page]) * PAGE).astype(F32)
        angle = position * freq
        cosine = jnp.cos(angle)
        sine = jnp.sin(angle)
        sine = jnp.where(lane < HD // 2, -sine, sine)
        for h in range(KVH):
            key = pkv[i * PAGE : (i + 1) * PAGE, h * 2 * HD : h * 2 * HD + HD].astype(F32)
            keys[i, h] = (key * cosine + pltpu.roll(key, HD // 2, 1) * sine).astype(BF)

    send(c7, nseq, me)

    arrive(c1, nseq, me)
    for t in range(nslice):
        for i in range(ppd):
            row = prow[(qbase + t) * ppd + i]
            stage2[t, i] = qall[row]
    send(c2, nslice, mine)
    q2[mine] = stage2[mine]
    kvall[me] = joined_ref[mine // steps, per_src * qn :]

    def fresh(tile, valid, q):
        sc = dot_t(q, tile) * scale
        sc = jnp.where(valid, sc, LOW)
        v = pltpu.roll(tile.astype(F32), 16 - steps, 0).astype(BF)
        return sc, v

    arrive(c5, KVH, head)
    col_c = lax.broadcasted_iota(jnp.int32, (qn, ctx), 1)
    col_s = lax.broadcasted_iota(jnp.int32, (qn, 16), 1)
    row_s = lax.broadcasted_iota(jnp.int32, (qn, 16), 0) // QPK

    def cached(r, c):
        load_c(r).wait()
        row = grp * rows + r
        length = jnp.where(rowp[row - quad * qrows] >= 0, 0, clen_ref[row])
        src, turn = r // per_src, r % per_src
        q = gq[src, pl.ds(pl.multiple_of(turn * qn, qn), qn)]
        sc = dot_t(q, cache[r, :, :HD]) * scale
        sc = jnp.where(col_c < length, sc, LOW)
        place = col_s - turn * 2 * steps
        sn, v = fresh(gq[src, per_src * qn :], (place >= 0) & (place <= row_s), q)
        top = jnp.maximum(jnp.max(sc, axis=-1, keepdims=True), jnp.max(sn, axis=-1, keepdims=True))
        e = jnp.exp(sc - top)
        en = jnp.exp(sn - top)
        total = jnp.sum(e, axis=-1, keepdims=True) + jnp.sum(en, axis=-1, keepdims=True)
        o = dot(e.astype(BF), cache[r, :, HD:]) + dot(en.astype(BF), v)
        res6[r] = (o / total).astype(BF)
        return c

    lax.fori_loop(0, rows // 2, cached, 0)

    lane_q = lax.broadcasted_iota(jnp.int32, (qn, HD), 1)
    def pages_of(h):
        for s in range(steps):
            @pl.when(h * steps + s != mine)
            def _():
                c2(mine, h * steps + s).wait_recv()
        packed = jnp.zeros((qn, HD), F32)
        for i in range(ppd):
            q = q2[h * steps : (h + 1) * steps, i].reshape(qn, HD)
            sc = dot_t(q, keys[i, h]) * scale
            top = jnp.max(sc, axis=-1, keepdims=True)
            e = jnp.exp(sc - top)
            total = jnp.sum(e, axis=-1, keepdims=True)
            v = pkv[i * PAGE : (i + 1) * PAGE, h * 2 * HD + HD : (h + 1) * 2 * HD]
            o = dot(e.astype(BF), v) / total
            stage3[h * steps : (h + 1) * steps, i] = o.astype(BF).reshape(steps, QPK, HD)
            x = jnp.broadcast_to(top + jnp.log(total), (qn, HD))
            packed = jnp.where(lane_q // 3 == i, x, packed)
        hi = packed.astype(BF).astype(F32)
        mid = (packed - hi).astype(BF).astype(F32)
        low = packed - hi - mid
        stat = jnp.where(lane_q % 3 == 0, hi, jnp.where(lane_q % 3 == 1, mid, low))
        stage3[h * steps : (h + 1) * steps, ppd] = stat.astype(BF).reshape(steps, QPK, HD)
        for block in range(nseq // nslice):
            for s in range(steps):
                t = block * nslice + h * steps + s
                @pl.when(t != me)
                def _():
                    c3(t, me).start()
    for plane in range(KVH):
        @pl.when(mine // steps == plane)
        def _():
            for k in (2, 1, 3, 0):
                pages_of((plane + k) % KVH)

    r3[me] = stage3[mine]

    arrive(c7, nseq, me)
    col_n = lax.broadcasted_iota(jnp.int32, (QPK, 16), 1)
    for p in range(nprompt):
        row = slot_ref[p]
        place = col_n - row % per_src * 2 * steps
        sc, v = fresh(kvall[row // per_src], (place >= 0) & (place <= step), qall[row])
        top = jnp.max(sc, axis=-1, keepdims=True)
        e = jnp.exp(sc - top)
        nmax[p] = jnp.broadcast_to(top, (QPK, HD))
        nsum[p] = jnp.broadcast_to(jnp.sum(e, axis=-1, keepdims=True), (QPK, HD))
        nacc[p] = dot(e.astype(BF), v)

    lax.fori_loop(rows // 2, rows, cached, 0)
    send(c6, KVH, head)
    r6[head] = res6[pl.ds(head * per_src, per_src)]

    arrive(c3, nseq, me)
    pick_r = lax.broadcasted_iota(jnp.int32, (HD, ppd * HD), 0)
    pick_c = lax.broadcasted_iota(jnp.int32, (HD, ppd * HD), 1)
    pick = jnp.where(pick_r // 3 == pick_c // HD, 1.0, 0.0).astype(BF)
    lse[...] = dot(r3[:, ppd].reshape(nseq * QPK, HD), pick)

    def at(g):
        return lse[g // ppd * QPK : (g // ppd + 1) * QPK, g % ppd * HD : (g % ppd + 1) * HD]

    opens = [pfirst[g] == g for g in range(npage)]
    drop = [jnp.where(o, F32(LOW), F32(0.0)) for o in opens]
    keep = [jnp.where(o, F32(0.0), F32(1.0)) for o in opens]
    for g in range(npage):
        run = at(g) if g == 0 else jnp.maximum(at(g), run + drop[g])
        fmax[g] = run
    for g in reversed(range(npage)):
        if g < npage - 1:
            run = jnp.maximum(fmax[g], run + drop[g + 1])
        fmax[g] = run
    for g in range(npage):
        w = jnp.exp(at(g) - fmax[g])
        o = r3[g // ppd, g % ppd].astype(F32) * w
        total = w if g == 0 else w + keep[g] * total
        acc = o if g == 0 else o + keep[g] * acc
        fsum[g] = total
        facc[g] = acc
    for p in range(nprompt):
        g = plast[p]
        top = jnp.maximum(fmax[g], nmax[p])
        a = jnp.exp(fmax[g] - top)
        b = jnp.exp(nmax[p] - top)
        fin[p] = ((facc[g] * a + nacc[p] * b) / (fsum[g] * a + nsum[p] * b)).astype(BF)
    for t in range(nslice):
        for i in range(per_src):
            stage4[t, i] = fin[jnp.maximum(rowp[t * per_src + i], 0)]
    send(c4, nslice, mine)
    r4[mine] = stage4[mine]

    arrive(c6, KVH, head)
    arrive(c4, nslice, mine)
    for i in range(per_src):
        has = rowp[mine * per_src + i]
        chosen = jnp.full((QPK, HD), has, jnp.int32) >= 0
        for h in range(KVH):
            for s in range(steps):
                a = r4[h * steps + s, i].astype(F32)
                b = r6[h, i, s * QPK : (s + 1) * QPK].astype(F32)
                out_ref[i, s, h * QPK : (h + 1) * QPK] = jnp.where(chosen, a, b).astype(BF)

    left(c1, nseq, me)
    left(c2, nslice, mine)
    left(c3, nseq, me)
    left(c4, nslice, mine)
    left(c5, KVH, head)
    left(c6, KVH, head)
    left(c7, nseq, me)


def per_device(prompt_kv, prompt_pages, prompt_slot, cache_kv, cache_len, queries, new_kv):
    nseq = lax.axis_size("seq")
    tok_dev = prompt_kv.shape[0]
    ppd = tok_dev // PAGE
    npage = ppd * nseq
    rows, ctx = cache_kv.shape[0], cache_kv.shape[1]
    per_src, steps = queries.shape[0], queries.shape[1]
    nprompt = prompt_pages.shape[0]
    nslice = KVH * steps
    qn = steps * QPK

    vmem = pl.BlockSpec(memory_space=pltpu.VMEM)
    hbm = pl.BlockSpec(memory_space=pl.ANY)
    V = pltpu.VMEM
    D = pltpu.SemaphoreType.DMA
    out = pl.pallas_call(
        functools.partial(kernel, nseq, steps, per_src, ppd, nprompt, ctx),
        out_shape=jax.ShapeDtypeStruct((per_src, steps, KVH * QPK, HD), BF),
        in_specs=[hbm] * 7,
        out_specs=vmem,
        scratch_shapes=[
            pltpu.SMEM(prompt_pages.shape, jnp.int32),
            pltpu.SMEM(prompt_slot.shape, jnp.int32),
            pltpu.SMEM(cache_len.shape, jnp.int32),
            pltpu.SMEM((npage,), jnp.int32),
            pltpu.SMEM((npage,), jnp.int32),
            pltpu.SMEM((nprompt,), jnp.int32),
            pltpu.SMEM((nslice * per_src,), jnp.int32),
            V(queries.shape, BF),
            V(new_kv.shape, BF),
            V((KVH, 16, HD), F32),
            V((KVH, per_src * qn + 16, HD), BF),
            V((tok_dev, KVH * 2 * HD), BF),
            V((rows, ctx, 2 * HD), BF),
            V((ppd, KVH, PAGE, HD), BF),
            V((nslice, per_src, QPK, HD), BF),
            V((nseq * per_src, QPK, HD), BF),
            V((nseq, 16, HD), BF),
            V((KVH, per_src * qn + 16, HD), BF),
            V((nslice, ppd, QPK, HD), BF),
            V((nslice, ppd, QPK, HD), BF),
            V((nslice, ppd + 1, QPK, HD), BF),
            V((nseq, ppd + 1, QPK, HD), BF),
            V((nseq * QPK, ppd * HD), F32),
            V((npage, QPK, HD), F32),
            V((npage, QPK, HD), F32),
            V((npage, QPK, HD), F32),
            V((nprompt, QPK, HD), F32),
            V((nprompt, QPK, HD), F32),
            V((nprompt, QPK, HD), F32),
            V((nprompt, QPK, HD), BF),
            V((nslice, per_src, QPK, HD), BF),
            V((nslice, per_src, QPK, HD), BF),
            V((rows, qn, HD), BF),
            V((KVH, per_src, qn, HD), BF),
            D((rows,)),
            D,
            D((5,)),
            D((nseq,)), D((nseq,)),
            D((nslice,)), D((nslice,)),
            D((nseq,)), D((nseq,)),
            D((nslice,)), D((nslice,)),
            D((KVH,)), D((KVH,)),
            D((KVH,)), D((KVH,)),
            D((nseq,)), D((nseq,)),
        ],
        compiler_params=pltpu.CompilerParams(
            collective_id=0, has_side_effects=True, vmem_limit_bytes=62 * 1024 * 1024
        ),
    )(prompt_pages, prompt_slot, cache_len, queries, new_kv, prompt_kv, cache_kv)
    return out.reshape(per_src, steps, KVH * QPK * HD)


def solution(mesh):
    placed = (
        P(("groups", "seq"), None),
        P("groups"),
        P("groups"),
        P(("groups", "seq"), None, None),
        P("groups"),
        P(("groups", "seq"), None, None),
        P(("groups", "seq"), None, None),
    )
    return jax.shard_map(
        per_device,
        mesh=mesh,
        in_specs=placed,
        out_specs=P(("groups", "seq"), None, None),
        check_vma=False,
    )
```
